128 devices in a mesh: dp: 2 (over x_hi), pipe: 8 (over z, core), tensor: 8 (over x_lo, y).
Axes of the slice: x: 4 (x_hi: 2, x_lo: 2; x = x_hi * 2 + x_lo), y: 4, z: 4, core: 2. Of those that a mesh axis runs over, the one named last changes fastest.
Arguments:
- tokens: bfloat16 [1024, 12288], P('pipe', ('dp', 'tensor')), may hold values from -6 to 6
- out_grad: bfloat16 [1024, 12288], P('pipe', ('dp', 'tensor')), may hold values from -6 to 6
- up_weight: bfloat16 [12288, 24576], P(('dp', 'tensor'), 'pipe'), may hold values from -0.0546875 to 0.0546875
- up_bias: float32 [24576], P('pipe'), may hold values from -5 to 5
- down_weight: bfloat16 [24576, 12288], P('pipe', ('dp', 'tensor')), may hold values from -0.0390625 to 0.0390625
Outputs:
- input_grad: bfloat16 [1024, 12288], P('pipe', ('dp', 'tensor'))
- up_weight_grad: bfloat16 [12288, 24576], P(('dp', 'tensor'), 'pipe')
- down_weight_grad: bfloat16 [24576, 12288], P('pipe', ('dp', 'tensor'))
- up_bias_grad: float32 [24576], P('pipe')
The draws below stay inside these ranges and needn't reach their ends.
All inputs are finite; a program needn't handle non-finite values.
Results may differ from the reference program's by a relative error of at most 0.029.
Values may be sent and summed in bfloat16 or wider, within the bound.
A program may use at most 128 MiB of HBM per device.

```python
import jax
import jax.numpy as jnp
from jax import lax

D = 12288
FH = 24576
TOK = 1024
N_DP = 2
N_TENSOR = 8


def level_of(own_key, shape, shards, least, largest):
    gain, own = 1.0, jax.random.fold_in(own_key, 6)
    for position, parts in shards:
        draws = jnp.exp(jax.random.uniform(jax.random.fold_in(own, position), (parts,), jnp.float32, least / len(shards), largest / len(shards)))
        gain = gain * jnp.repeat(draws, shape[position] // parts).reshape([-1 if axis == position else 1 for axis in range(len(shape))])
    return gain


def normal_values(key, extent, scale, reach, cuts=(), kind=jnp.bfloat16):
    gain = level_of(key, extent, cuts, -0.22, 0.18) if cuts else 1.0
    drawn = jax.random.normal(key, extent, jnp.float32) * scale * gain
    return jnp.minimum(jnp.maximum(drawn, -reach), reach).astype(kind)


def setup_inputs(seed: int = 0) -> dict:
    streams_of = jax.random.split(jax.random.key(seed), 6)
    return {
        "tokens": normal_values(streams_of[0], (TOK, D), 1.0, 6.0, ((0, 8), (1, 16))),
        "out_grad": normal_values(streams_of[1], (TOK, D), 1.0, 6.0, ((0, 8), (1, 16))),
        "up_weight": normal_values(streams_of[2], (D, FH), D ** -0.5, 0.0546875, ((0, 16), (1, 8))),
        "up_bias": normal_values(streams_of[3], (FH,), 1.0, 5.0, ((0, 8),), jnp.float32),
        "down_weight": normal_values(streams_of[4], (FH, D), FH ** -0.5, 0.0390625, ((0, 8), (1, 16))),
    }


def gelu_parts(value):
    coeff = 0.7978845608028654
    inner = coeff * (value + 0.044715 * value * value * value)
    tanh_val = jnp.tanh(inner)
    result = 0.5 * value * (1.0 + tanh_val)
    slope = 0.5 * (1.0 + tanh_val) + 0.5 * value * (1.0 - tanh_val * tanh_val) * coeff * (1.0 + 3.0 * 0.044715 * value * value)
    return result, slope


def reference(tokens, out_grad, up_weight, up_bias, down_weight):
    blocks = N_DP * N_TENSOR
    width = D // blocks
    across = (((1,), (1,)), ((), ()))
    preact = jnp.zeros((TOK, FH), jnp.float32)
    hidden_grad = jnp.zeros((TOK, FH), jnp.float32)
    for block in range(blocks):
        lower = block * width
        term = jnp.dot(tokens[:, lower:lower + width], up_weight[lower:lower + width, :], preferred_element_type=jnp.float32)
        term = lax.optimization_barrier(term.astype(jnp.bfloat16))
        preact = preact + term.astype(jnp.float32)
        back = lax.dot_general(out_grad[:, lower:lower + width], down_weight[:, lower:lower + width], across, preferred_element_type=jnp.float32)
        back = lax.optimization_barrier(back.astype(jnp.bfloat16))
        hidden_grad = hidden_grad + back.astype(jnp.float32)
    preact = preact + up_bias[None, :].astype(jnp.float32)
    result, slope = gelu_parts(preact)
    activation = result.astype(jnp.bfloat16)
    preact_grad = (hidden_grad * slope).astype(jnp.bfloat16)
    input_grad = lax.dot_general(preact_grad, up_weight, across, preferred_element_type=jnp.float32).astype(jnp.bfloat16)
    downward = (((0,), (0,)), ((), ()))
    up_weight_grad = lax.dot_general(tokens, preact_grad, downward, preferred_element_type=jnp.float32).astype(jnp.bfloat16)
    down_weight_grad = lax.dot_general(activation, out_grad, downward, preferred_element_type=jnp.float32).astype(jnp.bfloat16)
    up_bias_grad = jnp.sum(preact_grad.astype(jnp.float32), axis=0)
    return input_grad, up_weight_grad, down_weight_grad, up_bias_grad
```

```python
import jax
import jax.numpy as jnp
from jax import lax
from jax.experimental import pallas as pl
from jax.experimental.pallas import tpu as pltpu
from jax.sharding import PartitionSpec as P

MESH = pl.DeviceIdType.MESH
BF = jnp.bfloat16
F32 = jnp.float32
DB = 768
HB = 3072
OWN = 128
RG = 256
HC = 768
HH = HC // 2
NU = 16
DR = 5
DG = 8
LAST = 8


def gelu_parts(value):
    coeff = 0.7978845608028654
    inner = coeff * (value + 0.044715 * value * value * value)
    tanh_val = jnp.tanh(inner)
    result = 0.5 * value * (1.0 + tanh_val)
    slope = 0.5 * (1.0 + tanh_val) + 0.5 * value * (1.0 - tanh_val * tanh_val) * coeff * (
        1.0 + 3.0 * 0.044715 * value * value
    )
    return (result, slope)


def kernel(
    tok, og, w1h, bias, w2h,
    dx_out, dw1_out, dw2_out, db_out,
    xy, w1, w2, prod,
    mn1, mp1, kn1, kp1, kq1, lap1, lan1, lbp1, lbn1,
    mn2, mp2, kn2, kp2, kq2, lap2, lan2, lbp2, lbn2,
    gath,
    dxacc, dxl, dxs, dwacc, dwo, dxo,
    rss, rrs, gss, grs, xss, xrs, fss, frs, dss, drs, wsem, lsem, osem, dosem,
):
    t_ax = lax.axis_index("tensor")
    p_ax = lax.axis_index("pipe")
    x = lax.axis_index("dp") * 2 + t_ax // 4
    y = lax.rem(t_ax, 4)
    z = p_ax // 2
    c = lax.rem(p_ax, 2)

    def at_x(i):
        i = lax.rem(i + 4, 4)
        return {"dp": i // 2, "tensor": lax.rem(i, 2) * 4 + y}

    def at_y(j):
        return {"tensor": (x % 2) * 4 + lax.rem(j + 4, 4)}

    def at_z(k, core):
        return {"pipe": lax.rem(k + 4, 4) * 2 + core}

    ring_x = (x, at_x(x + 1), at_x(x - 1))
    ring_y = (y, at_y(y + 1), at_y(y - 1))
    sib = at_z(z, 1 - c)
    zs = (z, z + 1, z + 2, z - 1)
    back = (0, 3, 2, 1)

    bar = pltpu.get_barrier_semaphore()
    partners = [ring_x[1], ring_x[2], ring_y[1], ring_y[2], sib]
    for k in (1, 2, 3):
        for core in (0, 1):
            partners.append(at_z(zs[k], core))

    own_rows = pl.ds(pl.multiple_of(c * OWN, OWN), OWN)
    sib_rows = pl.ds(pl.multiple_of((1 - c) * OWN, OWN), OWN)

    def w_copy(which, g):
        cols = pl.ds(g * HC, HC)
        if which == 0:
            return pltpu.make_async_copy(w1h.at[:, cols], w1.at[g], wsem.at[0, g])
        return pltpu.make_async_copy(w2h.at[cols, :], w2.at[g], wsem.at[1, g])

    def local(which):
        return pltpu.make_async_copy((tok, og)[which], xy.at[which, 0, own_rows], lsem.at[which])

    local(0).start()
    local(1).start()
    for g in (1, 2, 3, 0):
        for which in (0, 1):
            w_copy(which, g).start()

    for d in partners:
        pl.semaphore_signal(bar, inc=1, device_id=d, device_id_type=MESH)
    pl.semaphore_wait(bar, len(partners))

    def remote(src, dst, ss, rs, device):
        return pltpu.make_async_remote_copy(
            src_ref=src, dst_ref=dst, send_sem=ss, recv_sem=rs, device_id=device, device_id_type=MESH
        )

    def x_copy(which, k):
        device = sib if k == 0 else at_z(zs[k], c)
        slot = back[k]
        return remote(
            (tok, og)[which], xy.at[which, slot, own_rows], xss.at[which, slot], xrs.at[which, slot], device
        )

    def x_forward(k):
        view = xy.at[:, k, own_rows]
        return remote(view, view, fss.at[k], frs.at[k], sib)

    for k in (0, 1, 3, 2):
        for which in (0, 1):
            x_copy(which, k).start()

    axes = ((ring_x, ring_y), (ring_y, ring_x))

    def rs_copy(slot, a, stage, hop, way):
        q, nxt, prv = axes[a][stage]
        src = (((mn1, mp1), (kn1, kp1)), ((mn2, mp2), (kn2, kp2)))[stage][hop][way]
        dst = (((lap1, lan1), (lbp1, lbn1)), ((lap2, lan2), (lbp2, lbn2)))[stage][hop][way]
        i = a * 8 + stage * 4 + hop * 2 + way
        return remote(src.at[slot, a], dst.at[slot, a], rss.at[slot, i], rrs.at[slot, i], (nxt, prv)[way])

    def ag_copy(slot, b, stage, hop, way):
        ring = axes[1 - b][stage]
        buf = gath.at[slot, b]
        q = ring[0]
        if hop == 1:
            q = lax.rem(q + (3 if way == 0 else 1), 4)
        along_x = (b == 0) == (stage == 1)
        if stage == 0:
            view = buf.at[q, y] if along_x else buf.at[x, q]
            if hop == 1:
                view = view.at[:, pl.ds(way * HH, HH)]
        else:
            part = pl.ds(0, 4) if hop == 0 else pl.ds(way * 2, 2)
            view = buf.at[q, part] if along_x else buf.at[part, q]
        i = b * 8 + stage * 4 + hop * 2 + way
        return remote(view, view, gss.at[slot, i], grs.at[slot, i], ring[1 + way])

    def each(make, op):
        for i in (0, 1):
            for way in (0, 1):
                getattr(make(i, way), op)()

    def unit(u):
        w = u + 1
        return lax.rem(w // 4, 4), lax.rem(w, 4)

    def f(v):
        return v.astype(F32)

    def add_into(ref, ix, other):
        ref[ix] = (f(ref[ix]) + f(other)).astype(BF)

    def produce(u):
        slot = lax.rem(u, DR)
        rg, cg = unit(u)
        prod[0] = (
            jnp.dot(xy[0, rg], w1[cg], preferred_element_type=F32).astype(BF).reshape(4, 4, 16, HC)
        )
        prod[1] = (
            lax.dot_general(xy[1, rg], w2[cg], (((1,), (1,)), ((), ())), preferred_element_type=F32)
            .astype(BF)
            .reshape(4, 4, 16, HC)
        )
        for a in (0, 1):
            q = axes[a][0][0]

            def stripe(r, k2):
                k1 = lax.rem(q + r, 4)
                return prod[a, k1, k2] if a == 0 else prod[a, k2, k1]

            for h in (0, 1):
                mn1[slot, a, 0, h] = stripe(2, h)
                mp1[slot, a, 0, h] = stripe(2, h + 2)
                mn1[slot, a, 1, h] = stripe(1, h + 2)
                kn1[slot, a, h] = stripe(1, h)
                mp1[slot, a, 1, h] = stripe(3, h)
                kp1[slot, a, h] = stripe(3, h + 2)
            for k2 in range(4):
                kq1[slot, a, k2] = stripe(0, k2)

    def stage0(u):
        slot = lax.rem(u, DR)
        each(lambda a, way: rs_copy(slot, a, 0, 0, way), "start")

    def stage1(u):
        slot = lax.rem(u, DR)
        for a in (0, 1):
            for way, (keep, land) in enumerate(((kn1, lap1), (kp1, lan1))):
                rs_copy(slot, a, 0, 0, way).wait()
                add_into(keep, (slot, a), land[slot, a, 0])
                rs_copy(slot, a, 0, 1, way).start()

    def stage2(u):
        slot = lax.rem(u, DR)
        for a in (0, 1):
            rs_copy(slot, a, 0, 1, 0).wait()
            rs_copy(slot, a, 0, 1, 1).wait()
            low, high = pl.ds(0, 2), pl.ds(2, 2)
            kq1[slot, a, low] = (
                f(kq1[slot, a, low]) + f(lan1[slot, a, 1]) + f(lbp1[slot, a])
            ).astype(BF)
            kq1[slot, a, high] = (
                f(kq1[slot, a, high]) + f(lap1[slot, a, 1]) + f(lbn1[slot, a])
            ).astype(BF)
            q = axes[a][1][0]

            def stripe(r):
                return kq1[slot, a, lax.rem(q + r, 4)]

            opposite, after, before = stripe(2), stripe(1), stripe(3)
            mn2[slot, a, 0] = opposite[:, :HH]
            mp2[slot, a, 0] = opposite[:, HH:]
            mn2[slot, a, 1] = after[:, HH:]
            kn2[slot, a] = after[:, :HH]
            mp2[slot, a, 1] = before[:, :HH]
            kp2[slot, a] = before[:, HH:]
            kq2[slot, a] = stripe(0)
            rs_copy(slot, a, 1, 0, 0).start()
            rs_copy(slot, a, 1, 0, 1).start()

    def stage3(u):
        slot = lax.rem(u, DR)
        for a in (0, 1):
            for way, (keep, land) in enumerate(((kn2, lap2), (kp2, lan2))):
                rs_copy(slot, a, 1, 0, way).wait()
                add_into(keep, (slot, a), land[slot, a, 0])
                rs_copy(slot, a, 1, 1, way).start()

    def stage4(u):
        slot = lax.rem(u, DR)
        gslot = lax.rem(u, DG)
        rg, cg = unit(u)
        each(lambda a, way: rs_copy(slot, a, 1, 1, way), "wait")
        for h, (direct, through) in enumerate(((lan2, lbp2), (lap2, lbn2))):
            cols = pl.ds(h * HH, HH)

            def whole(a):
                return f(kq2[slot, a, :, cols]) + f(direct[slot, a, 1]) + f(through[slot, a])

            preact = whole(0) + bias[cg, :, cols]
            result, slope = gelu_parts(preact)
            gath[gslot, 0, x, y, :, cols] = result.astype(BF)
            gath[gslot, 1, x, y, :, cols] = (whole(1) * slope).astype(BF)
        each(lambda b, way: ag_copy(gslot, b, 0, 0, way), "start")

    def gather_stage(u, stage, hop, next_stage, next_hop):
        slot = lax.rem(u, DG)
        each(lambda b, way: ag_copy(slot, b, stage, hop, way), "wait")
        if next_stage is not None:
            each(lambda b, way: ag_copy(slot, b, next_stage, next_hop, way), "start")

    def dx_copy(k, core):
        if k == 0:
            return remote(
                dxs.at[0, 1 - c], dxl.at[0, c], dss.at[0, 0], drs.at[0, c], sib
            )
        return remote(
            dxs.at[k, core], dxl.at[back[k], c], dss.at[k, core], drs.at[back[k], c], at_z(zs[k], core)
        )

    def dx_arrival(k, core):
        return pltpu.make_async_copy(dxl.at[k, core], dxl.at[k, core], drs.at[k, core])

    def dw_copy(which, cg):
        cols = pl.ds(pl.multiple_of(cg * HC, HC), HC)
        dst = dw1_out.at[:, cols] if which == 0 else dw2_out.at[cols, :]
        return pltpu.make_async_copy(dwo.at[which], dst, dosem.at[which])

    def consume(u):
        slot = lax.rem(u, DG)
        rg, cg = unit(u)
        grad = gath[slot, 1].reshape(RG, HC)
        mine = jnp.where(rg == 0, 0, 1)
        fresh = jnp.logical_or(u == 0, jnp.logical_and(cg == 0, rg != 0))

        @pl.when(fresh)
        def _():
            dxacc[mine] = jnp.zeros((RG, DB), F32)

        dxacc[mine] += lax.dot_general(
            grad, w1[cg], (((1,), (1,)), ((), ())), preferred_element_type=F32
        )

        @pl.when(jnp.logical_and(rg != 0, cg == 3))
        def _():
            dxs[rg] = dxacc[1].astype(BF).reshape(2, OWN, DB)
            for k in (1, 2, 3):

                @pl.when(rg == k)
                def _():
                    dx_copy(k, 0).start()
                    dx_copy(k, 1).start()

        @pl.when(u == NU - 1)
        def _():
            dxs[0] = dxacc[0].astype(BF).reshape(2, OWN, DB)
            dx_copy(0, 0).start()

        @pl.when(u < 4)
        def _():
            dwacc[cg] = jnp.zeros((2, DB, HC), F32)
            db_out[cg] = jnp.zeros((1, HC), F32)

        db_out[cg] += jnp.sum(f(grad), axis=0, keepdims=True)
        first = (((0,), (0,)), ((), ()))
        dwacc[cg, 0] += lax.dot_general(xy[0, rg], grad, first, preferred_element_type=F32)
        act = gath[slot, 0].reshape(RG, HC)
        dwacc[cg, 1] += lax.dot_general(act, xy[1, rg], first, preferred_element_type=F32)

        @pl.when(u >= NU - 4)
        def _():
            for which in (0, 1):

                @pl.when(u > NU - 4)
                def _():
                    dw_copy(which, cg).wait()

                dwo[which] = dwacc[cg, which].astype(BF)
                dw_copy(which, cg).start()

    def when_unit(u, body):
        @pl.when(jnp.logical_and(u >= 0, u < NU))
        def _():
            body(u)

    def tick(t, carry):
        when_unit(t, stage0)
        when_unit(t - 1, stage1)
        when_unit(t - 6, lambda u: gather_stage(u, 0, 1, 1, 0))
        when_unit(t - 7, lambda u: gather_stage(u, 1, 0, 1, 1))
        when_unit(t - 2, stage2)
        when_unit(t - 3, stage3)
        when_unit(t - 4, stage4)
        when_unit(t - 5, lambda u: gather_stage(u, 0, 0, 0, 1))

        for k, at in ((1, 1), (3, 2), (2, 3)):

            @pl.when(t == at)
            def _():
                for which in (0, 1):
                    x_copy(which, back[k]).wait_recv()
                x_forward(k).start()

        @pl.when(t == -1)
        def _():
            for which in (0, 1):
                local(which).wait()
                x_copy(which, 0).wait_recv()

        for k in (1, 2, 3):

            @pl.when(t + 1 == 4 * k - 1)
            def _():
                x_forward(k).wait_recv()

        for g in range(4):

            @pl.when(t + 1 == (g + 3) % 4)
            def _():
                w_copy(0, g).wait()
                w_copy(1, g).wait()

        when_unit(t + 1, produce)
        when_unit(t - LAST, lambda u: finish(u))
        return carry

    def finish(u):
        gather_stage(u, 1, 1, None, None)
        consume(u)

    lax.fori_loop(-1, NU + LAST, tick, 0)

    for k in (0, 1, 2, 3):
        for which in (0, 1):
            x_copy(which, k).wait_send()
    for k in (1, 2, 3):
        x_forward(k).wait_send()
    total = f(dxacc[0, own_rows])
    for k in (1, 2, 3):
        for core in (0, 1):
            dx_arrival(k, core).wait()
            total = total + f(dxl[k, core])
    dx_arrival(0, 1 - c).wait()
    total = total + f(dxl[0, 1 - c])
    dxo[...] = total.astype(BF)
    out = pltpu.make_async_copy(dxo, dx_out, osem)
    out.start()
    dx_copy(0, 0).wait_send()
    for k in (1, 2, 3):
        for core in (0, 1):
            dx_copy(k, core).wait_send()
    dw_copy(0, 0).wait()
    dw_copy(1, 0).wait()
    out.wait()


def body(tokens, out_grad, up_weight, up_bias, down_weight):
    hbm = pl.BlockSpec(memory_space=pl.ANY)
    vmem = pl.BlockSpec(memory_space=pltpu.VMEM)
    dma = pltpu.SemaphoreType.DMA
    bias = up_bias.reshape(4, 1, HC)

    def rs_scratch(*shape):
        return pltpu.VMEM((DR, 2) + shape, BF)

    first = [rs_scratch(2, 2, 16, HC)] * 2 + [rs_scratch(2, 16, HC)] * 2 + [rs_scratch(4, 16, HC)]
    first += [rs_scratch(2, 2, 16, HC)] * 2 + [rs_scratch(2, 16, HC)] * 2
    second = [rs_scratch(2, 16, HH)] * 2 + [rs_scratch(16, HH)] * 2 + [rs_scratch(16, HC)]
    second += [rs_scratch(2, 16, HH)] * 2 + [rs_scratch(16, HH)] * 2
    scratch = [
        pltpu.VMEM((2, 4, RG, DB), BF),
        pltpu.VMEM((4, DB, HC), BF),
        pltpu.VMEM((4, HC, DB), BF),
        pltpu.VMEM((2, 4, 4, 16, HC), BF),
        *first,
        *second,
        pltpu.VMEM((DG, 2, 4, 4, 16, HC), BF),
        pltpu.VMEM((2, RG, DB), F32),
        pltpu.VMEM((4, 2, OWN, DB), BF),
        pltpu.VMEM((4, 2, OWN, DB), BF),
        pltpu.VMEM((4, 2, DB, HC), F32),
        pltpu.VMEM((2, DB, HC), BF),
        pltpu.VMEM((OWN, DB), BF),
        dma((DR, 16)),
        dma((DR, 16)),
        dma((DG, 16)),
        dma((DG, 16)),
        dma((2, 4)),
        dma((2, 4)),
        dma((4,)),
        dma((4,)),
        dma((4, 2)),
        dma((4, 2)),
        dma((2, 4)),
        dma((2,)),
        dma(()),
        dma((2,)),
    ]
    dx, dw1, dw2, db = pl.pallas_call(
        kernel,
        out_shape=(
            jax.ShapeDtypeStruct((OWN, DB), BF),
            jax.ShapeDtypeStruct((DB, HB), BF),
            jax.ShapeDtypeStruct((HB, DB), BF),
            jax.ShapeDtypeStruct((4, 1, HC), F32),
        ),
        in_specs=[hbm, hbm, hbm, vmem, hbm],
        out_specs=(hbm, hbm, hbm, vmem),
        scratch_shapes=scratch,
        compiler_params=pltpu.CompilerParams(
            collective_id=0, has_side_effects=True, vmem_limit_bytes=62 * 2**20
        ),
        cost_estimate=pl.CostEstimate(
            flops=10 * 1024 * DB * HB, bytes_accessed=20 * 2**20, transcendentals=1024 * HB // 16
        ),
    )(tokens, out_grad, up_weight, bias, down_weight)
    return (dx, dw1, dw2, db.reshape(HB))


def solution(mesh):
    placed = (
        P("pipe", ("dp", "tensor")),
        P("pipe", ("dp", "tensor")),
        P(("dp", "tensor"), "pipe"),
        P("pipe"),
        P("pipe", ("dp", "tensor")),
    )
    return jax.shard_map(
        body,
        mesh=mesh,
        in_specs=placed,
        out_specs=(
            P("pipe", ("dp", "tensor")),
            P(("dp", "tensor"), "pipe"),
            P("pipe", ("dp", "tensor")),
            P("pipe"),
        ),
        check_vma=False,
    )
```

```python
import jax
import jax.numpy as jnp
from jax import lax
from jax.experimental import pallas as pl
from jax.experimental.pallas import tpu as pltpu
from jax.sharding import PartitionSpec as P

MESH = pl.DeviceIdType.MESH
BF = jnp.bfloat16
F32 = jnp.float32
DB = 768
HB = 3072
OWN = 128
RG = 256
HC = 768
HH = HC // 2
NU = 16
DR = 5
DG = 7
DM = 3
DK = 4
LAST = 8


def gelu_parts(value):
    coeff = 0.7978845608028654
    inner = coeff * (value + 0.044715 * value * value * value)
    tanh_val = jnp.tanh(inner)
    result = 0.5 * value * (1.0 + tanh_val)
    slope = 0.5 * (1.0 + tanh_val) + 0.5 * value * (1.0 - tanh_val * tanh_val) * coeff * (
        1.0 + 3.0 * 0.044715 * value * value
    )
    return (result, slope)


def kernel(
    tok, og, w1h, bias_h, w2h,
    dx_out, dw1_out, dw2_out, db_out,
    xy, w1, w2, bias, prod,
    mn1, mp1, kn1, kp1, kq1, lap1, lan1, lbp1, lbn1,
    mn2, mp2, kn2, kp2, kq2, lap2, lan2, lbp2, lbn2,
    gath,
    dxacc, dxl, dxs, dwacc,
    rss, rrs, gss, grs, xss, xrs, fss, frs, dss, drs, wsem, lsem, bsem,
):
    t_ax = lax.axis_index("tensor")
    p_ax = lax.axis_index("pipe")
    x = lax.axis_index("dp") * 2 + t_ax // 4
    y = lax.rem(t_ax, 4)
    z = p_ax // 2
    c = lax.rem(p_ax, 2)

    def at_x(i):
        i = lax.rem(i + 4, 4)
        return {"dp": i // 2, "tensor": lax.rem(i, 2) * 4 + y}

    def at_y(j):
        return {"tensor": (x % 2) * 4 + lax.rem(j + 4, 4)}

    def at_z(k, core):
        return {"pipe": lax.rem(k + 4, 4) * 2 + core}

    ring_x = (x, at_x(x + 1), at_x(x - 1))
    ring_y = (y, at_y(y + 1), at_y(y - 1))
    sib = at_z(z, 1 - c)
    zs = (z, z + 1, z + 2, z - 1)
    back = (0, 3, 2, 1)
    direct_group = 1 + 2 * c

    bar = pltpu.get_barrier_semaphore()
    partners = [ring_x[1], ring_x[2], ring_y[1], ring_y[2], sib]
    for k in (1, 2, 3):
        for core in (0, 1):
            partners.append(at_z(zs[k], core))

    own_rows = pl.ds(pl.multiple_of(c * OWN, OWN), OWN)
    sib_rows = pl.ds(pl.multiple_of((1 - c) * OWN, OWN), OWN)

    def w_copy(which, g):
        cols = pl.ds(g * HC, HC)
        if which == 0:
            return pltpu.make_async_copy(w1h.at[:, cols], w1.at[g], wsem.at[0, g])
        return pltpu.make_async_copy(w2h.at[cols, :], w2.at[g], wsem.at[1, g])

    def local(which):
        return pltpu.make_async_copy((tok, og)[which], xy.at[which, 0, own_rows], lsem.at[which])

    bias_copy = pltpu.make_async_copy(bias_h, bias, bsem)
    local(0).start()
    local(1).start()
    for g in (1, 2, 3, 0):
        for which in (0, 1):
            w_copy(which, g).start()
    bias_copy.start()

    for d in partners:
        pl.semaphore_signal(bar, inc=1, device_id=d, device_id_type=MESH)
    pl.semaphore_wait(bar, len(partners))

    def remote(src, dst, ss, rs, device):
        return pltpu.make_async_remote_copy(
            src_ref=src, dst_ref=dst, send_sem=ss, recv_sem=rs, device_id=device, device_id_type=MESH
        )

    def x_copy(which, k):
        if k == 0:
            dst = xy.at[which, 0, own_rows]
        elif k == 2:
            dst = xy.at[which, 2, own_rows]
        else:
            dst = xy.at[which, direct_group, pl.ds(OWN * (k == 1), OWN)]
        slot = back[k]
        device = sib if k == 0 else at_z(zs[k], c)
        return remote((tok, og)[which], dst, xss.at[which, slot], xrs.at[which, slot], device)

    def x_forward(which, k):
        view = xy.at[which, 2, own_rows] if k == 2 else xy.at[which, direct_group]
        return remote(view, view, fss.at[which, k], frs.at[which, k], sib)

    def x_forwarded(k):
        x_forward(0, k).wait_recv()
        x_forward(1, k).wait_recv()

    def x_start(*ks):
        for which in (0, 1):
            for k in ks:
                x_copy(which, k).start()

    def x_relay(which, k):
        for slot in (2,) if k == 2 else (1, 3):
            x_copy(which, back[slot]).wait_recv()
        x_forward(which, k).start()

    def x_relay_both(k):
        x_relay(0, k)
        x_relay(1, k)

    x_start(0)

    @pl.when(c == 0)
    def _():
        x_start(1, 3)

    axes = ((ring_x, ring_y), (ring_y, ring_x))

    def rs_copy(u, a, stage, hop, way):
        slot = lax.rem(u, DR)
        held = slot if stage == 1 else lax.rem(u, DK if hop == 1 else DM)
        _, nxt, prv = axes[a][stage]
        src = (((mn1, mp1), (kn1, kp1)), ((mn2, mp2), (kn2, kp2)))[stage][hop][way]
        dst = (((lap1, lan1), (lbp1, lbn1)), ((lap2, lan2), (lbp2, lbn2)))[stage][hop][way]
        i = a * 8 + stage * 4 + hop * 2 + way
        return remote(src.at[held, a], dst.at[slot, a], rss.at[slot, i], rrs.at[slot, i], (nxt, prv)[way])

    def ag_copy(slot, b, stage, hop, way):
        ring = axes[1 - b][stage]
        buf = gath.at[slot, b]
        q = ring[0]
        if hop == 1:
            q = lax.rem(q + (3 if way == 0 else 1), 4)
        along_x = (b == 0) == (stage == 1)
        if stage == 0:
            view = buf.at[q, y] if along_x else buf.at[x, q]
            if hop == 1:
                view = view.at[:, pl.ds(way * HH, HH)]
        else:
            part = pl.ds(0, 4) if hop == 0 else pl.ds(way * 2, 2)
            view = buf.at[q, part] if along_x else buf.at[part, q]
        i = b * 8 + stage * 4 + hop * 2 + way
        return remote(view, view, gss.at[slot, i], grs.at[slot, i], ring[1 + way])

    def each(make, op):
        for i in (0, 1):
            for way in (0, 1):
                getattr(make(i, way), op)()

    def unit(u):
        w = u + 1
        return lax.rem(w // 4, 4), lax.rem(w, 4)

    def f(v):
        return v.astype(F32)

    def add_into(ref, ix, other):
        ref[ix] = (f(ref[ix]) + f(other)).astype(BF)

    def produce(u):
        sent, held = lax.rem(u, DM), lax.rem(u, DK)
        rg, cg = unit(u)
        for a in (0, 1):
            inner = (((1,), (a,)), ((), ()))
            weight = (w1, w2)[a][cg]
            prod[...] = (
                lax.dot_general(xy[a, rg], weight, inner, preferred_element_type=F32)
                .astype(BF)
                .reshape(4, 4, 16, HC)
            )
            q = axes[a][0][0]

            def stripe(r, k2):
                k1 = lax.rem(q + r, 4)
                return prod[k1, k2] if a == 0 else prod[k2, k1]

            for h in (0, 1):
                mn1[sent, a, 0, h] = stripe(2, h)
                mp1[sent, a, 0, h] = stripe(2, h + 2)
                mn1[sent, a, 1, h] = stripe(1, h + 2)
                kn1[held, a, h] = stripe(1, h)
                mp1[sent, a, 1, h] = stripe(3, h)
                kp1[held, a, h] = stripe(3, h + 2)
            for k2 in range(4):
                kq1[held, a, k2] = stripe(0, k2)

    def stage0(u):
        each(lambda a, way: rs_copy(u, a, 0, 0, way), "start")

    def stage1(u):
        slot, held = lax.rem(u, DR), lax.rem(u, DK)
        for a in (0, 1):
            for way, (keep, land) in enumerate(((kn1, lap1), (kp1, lan1))):
                rs_copy(u, a, 0, 0, way).wait()
                add_into(keep, (held, a), land[slot, a, 0])
                rs_copy(u, a, 0, 1, way).start()

    def stage2(u):
        slot, held = lax.rem(u, DR), lax.rem(u, DK)
        for a in (0, 1):
            rs_copy(u, a, 0, 1, 0).wait()
            rs_copy(u, a, 0, 1, 1).wait()
            low, high = pl.ds(0, 2), pl.ds(2, 2)
            kq1[held, a, low] = (
                f(kq1[held, a, low]) + f(lan1[slot, a, 1]) + f(lbp1[slot, a])
            ).astype(BF)
            kq1[held, a, high] = (
                f(kq1[held, a, high]) + f(lap1[slot, a, 1]) + f(lbn1[slot, a])
            ).astype(BF)
            q = axes[a][1][0]

            def stripe(r):
                return kq1[held, a, lax.rem(q + r, 4)]

            opposite, after, before = stripe(2), stripe(1), stripe(3)
            mn2[slot, a, 0] = opposite[:, :HH]
            mp2[slot, a, 0] = opposite[:, HH:]
            mn2[slot, a, 1] = after[:, HH:]
            kn2[slot, a] = after[:, :HH]
            mp2[slot, a, 1] = before[:, :HH]
            kp2[slot, a] = before[:, HH:]
            kq2[slot, a] = stripe(0)
            rs_copy(u, a, 1, 0, 0).start()
            rs_copy(u, a, 1, 0, 1).start()

    def stage3(u):
        slot = lax.rem(u, DR)
        for a in (0, 1):
            for way, (keep, land) in enumerate(((kn2, lap2), (kp2, lan2))):
                rs_copy(u, a, 1, 0, way).wait()
                add_into(keep, (slot, a), land[slot, a, 0])
                rs_copy(u, a, 1, 1, way).start()

    def stage4(u):
        slot = lax.rem(u, DR)
        gslot = lax.rem(u, DG)
        rg, cg = unit(u)
        each(lambda a, way: rs_copy(u, a, 1, 1, way), "wait")
        for h, (direct, through) in enumerate(((lan2, lbp2), (lap2, lbn2))):
            cols = pl.ds(h * HH, HH)

            def whole(a):
                return f(kq2[slot, a, :, cols]) + f(direct[slot, a, 1]) + f(through[slot, a])

            preact = whole(0) + bias[cg, :, cols]
            result, slope = gelu_parts(preact)
            gath[gslot, 0, x, y, :, cols] = result.astype(BF)
            gath[gslot, 1, x, y, :, cols] = (whole(1) * slope).astype(BF)
        each(lambda b, way: ag_copy(gslot, b, 0, 0, way), "start")

    def gather_stage(u, stage, hop, next_stage, next_hop):
        slot = lax.rem(u, DG)
        each(lambda b, way: ag_copy(slot, b, stage, hop, way), "wait")
        if next_stage is not None:
            each(lambda b, way: ag_copy(slot, b, next_stage, next_hop, way), "start")

    def dx_copy(k, h):
        if k == 0:
            device, slot, src = sib, 0, dxs.at[0, 1 - c]
        elif k == 2:
            device, slot, src = at_z(zs[2], h), 2, dxs.at[0, h]
        else:
            device, slot, src = at_z(zs[1 + 2 * h], k // 2), 3 - 2 * h, dxs.at[1, h]
        return remote(src, dxl.at[slot, c], dss.at[k, h], drs.at[slot, c], device)

    def dx_sent(k):
        dx_copy(k, 0).wait_send()
        dx_copy(k, 1).wait_send()

    def dx_arrival(k, core):
        return pltpu.make_async_copy(dxl.at[k, core], dxl.at[k, core], drs.at[k, core])

    def consume(u):
        slot = lax.rem(u, DG)
        rg, cg = unit(u)
        grad = gath[slot, 1].reshape(RG, HC)
        mine = jnp.where(rg == 0, 0, 1)
        fresh = jnp.logical_or(u == 0, jnp.logical_and(cg == 0, rg != 0))

        @pl.when(fresh)
        def _():
            dxacc[mine] = jnp.zeros((RG, DB), F32)

        dxacc[mine] += lax.dot_general(
            grad, w1[cg], (((1,), (1,)), ((), ())), preferred_element_type=F32
        )

        for k, done in ((1, 6), (2, 10), (3, 14), (0, NU - 1)):

            @pl.when(u == done)
            def _():
                if k in (3, 0):
                    dx_sent({3: 1, 0: 2}[k])
                dxs[k % 2] = dxacc[min(k, 1)].astype(BF).reshape(2, OWN, DB)
                dx_copy(k, 0).start()
                if k != 0:
                    dx_copy(k, 1).start()

        @pl.when(u < 4)
        def _():
            dwacc[cg] = jnp.zeros((2, DB, HC), F32)
            db_out[cg] = jnp.zeros((1, HC), F32)

        db_out[cg] += jnp.sum(f(grad), axis=0, keepdims=True)
        first = (((0,), (0,)), ((), ()))
        dwacc[cg, 0] += lax.dot_general(xy[0, rg], grad, first, preferred_element_type=F32)
        act = gath[slot, 0].reshape(RG, HC)
        dwacc[cg, 1] += lax.dot_general(act, xy[1, rg], first, preferred_element_type=F32)

        @pl.when(u >= NU - 4)
        def _():
            cols = pl.ds(pl.multiple_of(cg * HC, HC), HC)
            dw1_out[:, cols] = dwacc[cg, 0].astype(BF)
            dw2_out[cols, :] = dwacc[cg, 1].astype(BF)

    def when_unit(u, body):
        @pl.when(jnp.logical_and(u >= 0, u < NU))
        def _():
            body(u)

    def tick(t, carry):
        def at(when, core=None):
            hit = t == when
            return pl.when(hit if core is None else jnp.logical_and(hit, c == core))

        when_unit(t, stage0)
        at(0, 0)(lambda: x_relay(0, 1))
        at(1, 0)(lambda: x_relay(1, 1))
        when_unit(t - 1, stage1)
        when_unit(t - 2, stage2)
        when_unit(t - 3, stage3)
        when_unit(t - 4, stage4)
        when_unit(t - 5, lambda u: gather_stage(u, 0, 0, 0, 1))
        when_unit(t - 6, lambda u: gather_stage(u, 0, 1, 1, 0))
        when_unit(t - 7, lambda u: gather_stage(u, 1, 0, 1, 1))

        @at(-1)
        def _():
            bias_copy.wait()
            for which in (0, 1):
                local(which).wait()
                x_copy(which, 0).wait_recv()

        at(2)(lambda: x_start(2))
        at(2, 1)(lambda: x_forwarded(1))
        at(4, 1)(lambda: x_start(1, 3))
        at(5)(lambda: x_relay_both(2))
        at(6)(lambda: x_forwarded(2))
        at(8, 1)(lambda: x_relay_both(1))
        at(10, 0)(lambda: x_forwarded(1))

        for g in range(4):

            @pl.when(t + 1 == (g + 3) % 4)
            def _():
                w_copy(0, g).wait()
                w_copy(1, g).wait()

        when_unit(t + 1, produce)
        when_unit(t - LAST, lambda u: finish(u))
        return carry

    def finish(u):
        gather_stage(u, 1, 1, None, None)
        consume(u)

    lax.fori_loop(-1, NU + LAST, tick, 0)

    for k in (0, 1, 2, 3):
        for which in (0, 1):
            x_copy(which, k).wait_send()
    for k in (1, 2):
        x_forward(0, k).wait_send()
        x_forward(1, k).wait_send()
    total = f(dxacc[0, own_rows])
    for k in (1, 2, 3):
        for core in (0, 1):
            dx_arrival(k, core).wait()
            total = total + f(dxl[k, core])
    dx_arrival(0, 1 - c).wait()
    total = total + f(dxl[0, 1 - c])
    dx_out[...] = total.astype(BF)
    dx_copy(0, 0).wait_send()
    dx_sent(3)


def store(*refs):
    count = len(refs) // 2
    sem = refs[-1]
    copies = [pltpu.make_async_copy(refs[i], refs[count + i], sem.at[i]) for i in range(count)]
    for copy in copies:
        copy.start()
    for copy in copies:
        copy.wait()


def body(tokens, out_grad, up_weight, up_bias, down_weight):
    hbm = pl.BlockSpec(memory_space=pl.ANY)
    vmem = pl.BlockSpec(memory_space=pltpu.VMEM)
    dma = pltpu.SemaphoreType.DMA
    bias = up_bias.reshape(4, 1, HC)
    shapes = (((OWN, DB), BF), ((DB, HB), BF), ((HB, DB), BF), ((4, 1, HC), F32))

    def rs_scratch(*shape):
        return pltpu.VMEM((DR, 2) + shape, BF)

    first = [pltpu.VMEM((DM, 2, 2, 2, 16, HC), BF)] * 2 + [pltpu.VMEM((DK, 2, 2, 16, HC), BF)] * 2
    first += [pltpu.VMEM((DK, 2, 4, 16, HC), BF)]
    first += [rs_scratch(2, 2, 16, HC)] * 2 + [rs_scratch(2, 16, HC)] * 2
    second = [rs_scratch(2, 16, HH)] * 2 + [rs_scratch(16, HH)] * 2 + [rs_scratch(16, HC)]
    second += [rs_scratch(2, 16, HH)] * 2 + [rs_scratch(16, HH)] * 2
    scratch = [
        pltpu.VMEM((2, 4, RG, DB), BF),
        pltpu.VMEM((4, DB, HC), BF),
        pltpu.VMEM((4, HC, DB), BF),
        pltpu.VMEM((4, 1, HC), F32),
        pltpu.VMEM((4, 4, 16, HC), BF),
        *first,
        *second,
        pltpu.VMEM((DG, 2, 4, 4, 16, HC), BF),
        pltpu.VMEM((2, RG, DB), F32),
        pltpu.VMEM((4, 2, OWN, DB), BF),
        pltpu.VMEM((2, 2, OWN, DB), BF),
        pltpu.VMEM((4, 2, DB, HC), F32),
        dma((DR, 16)),
        dma((DR, 16)),
        dma((DG, 16)),
        dma((DG, 16)),
        dma((2, 4)),
        dma((2, 4)),
        dma((2, 4)),
        dma((2, 4)),
        dma((4, 2)),
        dma((4, 2)),
        dma((2, 4)),
        dma((2,)),
        dma(()),
    ]
    results = pl.pallas_call(
        kernel,
        out_shape=tuple(pltpu.VMEM(shape, dtype) for shape, dtype in shapes),
        in_specs=[hbm] * 5,
        out_specs=(vmem,) * 4,
        scratch_shapes=scratch,
        compiler_params=pltpu.CompilerParams(
            collective_id=0, has_side_effects=True, vmem_limit_bytes=53 * 2**20
        ),
        cost_estimate=pl.CostEstimate(
            flops=10 * 1024 * DB * HB, bytes_accessed=20 * 2**20, transcendentals=1024 * HB // 16
        ),
    )(tokens, out_grad, up_weight, bias, down_weight)
    dx, dw1, dw2, db = pl.pallas_call(
        store,
        out_shape=tuple(jax.ShapeDtypeStruct(shape, dtype) for shape, dtype in shapes),
        in_specs=[hbm] * 4,
        out_specs=(hbm,) * 4,
        scratch_shapes=[dma((4,))],
        compiler_params=pltpu.CompilerParams(vmem_limit_bytes=2**22),
    )(*(pltpu.with_memory_space_constraint(a, pltpu.VMEM) for a in results))
    return (dx, dw1, dw2, db.reshape(HB))


def solution(mesh):
    placed = (
        P("pipe", ("dp", "tensor")),
        P("pipe", ("dp", "tensor")),
        P(("dp", "tensor"), "pipe"),
        P("pipe"),
        P("pipe", ("dp", "tensor")),
    )
    return jax.shard_map(
        body,
        mesh=mesh,
        in_specs=placed,
        out_specs=(
            P("pipe", ("dp", "tensor")),
            P(("dp", "tensor"), "pipe"),
            P("pipe", ("dp", "tensor")),
            P("pipe"),
        ),
        check_vma=False,
    )
```
